32 devices in a mesh: grp: 2 (over y), hid: 4 (over z), wid: 2 (over x), dat: 2 (over core).
Axes of the slice: x: 2, y: 2, z: 4, core: 2. Of those that a mesh axis runs over, the one named last changes fastest.
Arguments:
- tokens: bfloat16 [128, 4096], P(('grp', 'hid', 'dat'), 'wid'), parts along dimension 0, may hold values from -6 to 6
- output_gradient: bfloat16 [128, 4096], P(('grp', 'hid', 'dat'), 'wid'), parts along dimension 0, may hold values from -6 to 6
- gate_weight_blocks: bfloat16 [4, 2, 48, 128, 128], P('hid', 'wid'), may hold values from -0.125 to 0.125
- gate_block_places: int32 [4, 2, 48], P('hid', 'wid'), may hold values from 0 to 64, as said below
- up_weight_blocks: bfloat16 [4, 2, 48, 128, 128], P('hid', 'wid'), may hold values from -0.125 to 0.125
- up_block_places: int32 [4, 2, 48], P('hid', 'wid'), may hold values from 0 to 64, as said below
- down_weight_blocks: bfloat16 [4, 2, 48, 128, 128], P('hid', 'wid'), may hold values from -0.1875 to 0.1875
- down_block_places: int32 [4, 2, 48], P('hid', 'wid'), may hold values from 0 to 64, as said below
- gate_adapter_first: bfloat16 [4096, 16], P('wid'), may hold values from -0.09375 to 0.09375
- gate_adapter_second: bfloat16 [16, 2048], P(None, 'hid'), may hold values from -0.59765625 to 0.59765625
- up_adapter_first: bfloat16 [4096, 16], P('wid'), may hold values from -0.09375 to 0.09375
- up_adapter_second: bfloat16 [16, 2048], P(None, 'hid'), may hold values from -0.59765625 to 0.59765625
- down_adapter_first: bfloat16 [2048, 16], P('hid'), may hold values from -0.125 to 0.125
- down_adapter_second: bfloat16 [16, 4096], P(None, 'wid'), may hold values from -0.29882812 to 0.29882812
Outputs:
- token_gradient: bfloat16 [128, 4096], P(('grp', 'hid', 'dat'), 'wid'), parts along dimension 0
- gate_adapter_gradient: float32 [32, 2048], P('grp', 'hid'), parts along dimension 0
- up_adapter_gradient: float32 [32, 2048], P('grp', 'hid'), parts along dimension 0
- down_adapter_gradient: float32 [32, 4096], P('grp', 'wid'), parts along dimension 0
The draws below stay inside these ranges and needn't reach their ends.
There are 2 independent parts, one for each index of `grp`. The reference program is written for one: setup_inputs(seed, part) draws one part's arguments, and reference() takes and returns one part's arrays. A program takes and returns all parts, laid end to end along the dimension named above; an argument that names none is the same for every part. Nothing has to cross between parts.
Inputs may be any that keep to these rules, and one draw needn't show every extreme that they name: `gate_block_places`: in each tile the live slots come first and name distinct block positions; the remaining slots hold 64. Some tile of the matrix has all 48 slots live. `up_block_places`: as for gate_block_places. `down_block_places`: as for gate_block_places.
All inputs are finite; a program needn't handle non-finite values.
Results may differ from the reference program's by a relative error of at most 0.0049.
Values may be sent and summed in bfloat16 or wider, within the bound.
A program may use at most 64 MiB of HBM per device.

```python
import jax
import jax.numpy as jnp
from jax import lax

BLOCK = 128
HB_DEV = 4
WB_DEV = 16
CAP = 48
ADAPTER_RANK = 16
MODEL_WIDTH = 4096
HIDDEN_UNITS = 2048
TOKENS = 64
N_HID = 4
N_WID = 2


def slot_table(key):
    count_key, shuffle_key, full_key = jax.random.split(key, 3)
    tile_total = N_HID * N_WID
    positions = HB_DEV * WB_DEV
    counts = jax.random.randint(count_key, (tile_total,), positions - CAP, CAP + 1)
    full_tile = jax.random.randint(full_key, (), 0, tile_total)
    counts = jnp.where(jnp.arange(tile_total) == full_tile, CAP, counts)
    shuffled = jax.vmap(lambda single: jax.random.permutation(single, positions))(jax.random.split(shuffle_key, tile_total))[:, :CAP]
    table = jnp.where(jnp.arange(CAP)[None, :] < counts[:, None], shuffled, positions)
    return table.reshape(N_HID, N_WID, CAP).astype(jnp.int32)


def draw_gate_block_places(key, part):
    key = jax.random.fold_in(key, 11)
    return slot_table(key)


def draw_up_block_places(key, part):
    key = jax.random.fold_in(key, 23)
    return slot_table(key)


def draw_down_block_places(key, part):
    key = jax.random.fold_in(key, 37)
    return slot_table(key)


def steps_of(own_key, dims, pieces, low, top_value):
    def one(position, blocks):
        draws = jax.random.uniform(jax.random.fold_in(jax.random.fold_in(own_key, 6), position), (blocks,), jnp.float32, low / len(pieces), top_value / len(pieces))
        return jnp.repeat(jnp.exp(draws), dims[position] // blocks).reshape((-1,) + (1,) * (len(dims) - position - 1))

    loudness = one(*pieces[0])
    for cut in pieces[1:]:
        loudness = loudness * one(*cut)
    return loudness


def gaussian(key, dims, scale, most, cuts=(), dtype=jnp.bfloat16):
    result = scale * jax.random.normal(key, dims, jnp.float32)
    if cuts:
        result = result * steps_of(key, dims, cuts, -0.22, 0.18)
    return jnp.clip(result, -most, most).astype(dtype)


def setup_inputs(seed: int = 0, part: int = 0) -> dict:
    arg_keys = jax.random.split(jax.random.key(seed), 15)
    part_splits = jax.random.split(jax.random.fold_in(arg_keys[14], part), 15)
    tokens = gaussian(part_splits[0], (TOKENS, MODEL_WIDTH), 1.0, 6.0, ((0, 8), (1, 2)))
    output_gradient = gaussian(part_splits[1], (TOKENS, MODEL_WIDTH), 1.0, 6.0, ((0, 8), (1, 2)))
    gate_weight_blocks = gaussian(arg_keys[2], (N_HID, N_WID, CAP, BLOCK, BLOCK), (MODEL_WIDTH // 2) ** -0.5, 0.125, ((0, 4), (1, 2)))
    gate_block_places = draw_gate_block_places(jax.random.fold_in(arg_keys[14], 71), part)
    up_weight_blocks = gaussian(arg_keys[4], (N_HID, N_WID, CAP, BLOCK, BLOCK), (MODEL_WIDTH // 2) ** -0.5, 0.125, ((0, 4), (1, 2)))
    up_block_places = draw_up_block_places(jax.random.fold_in(arg_keys[14], 71), part)
    down_weight_blocks = gaussian(arg_keys[6], (N_HID, N_WID, CAP, BLOCK, BLOCK), (HIDDEN_UNITS // 2) ** -0.5, 0.1875, ((0, 4), (1, 2)))
    down_block_places = draw_down_block_places(jax.random.fold_in(arg_keys[14], 71), part)
    gate_adapter_first = gaussian(arg_keys[8], (MODEL_WIDTH, ADAPTER_RANK), MODEL_WIDTH ** -0.5, 0.09375, ((0, 2),))
    gate_adapter_second = gaussian(arg_keys[9], (ADAPTER_RANK, HIDDEN_UNITS), 0.1, 0.59765625, ((1, 4),))
    up_adapter_first = gaussian(arg_keys[10], (MODEL_WIDTH, ADAPTER_RANK), MODEL_WIDTH ** -0.5, 0.09375, ((0, 2),))
    up_adapter_second = gaussian(arg_keys[11], (ADAPTER_RANK, HIDDEN_UNITS), 0.1, 0.59765625, ((1, 4),))
    down_adapter_first = gaussian(arg_keys[12], (HIDDEN_UNITS, ADAPTER_RANK), HIDDEN_UNITS ** -0.5, 0.125, ((0, 4),))
    down_adapter_second = gaussian(arg_keys[13], (ADAPTER_RANK, MODEL_WIDTH), 0.05, 0.29882812, ((1, 2),))
    return dict(tokens=tokens, output_gradient=output_gradient, gate_weight_blocks=gate_weight_blocks, gate_block_places=gate_block_places, up_weight_blocks=up_weight_blocks, up_block_places=up_block_places, down_weight_blocks=down_weight_blocks, down_block_places=down_block_places, gate_adapter_first=gate_adapter_first, gate_adapter_second=gate_adapter_second, up_adapter_first=up_adapter_first, up_adapter_second=up_adapter_second, down_adapter_first=down_adapter_first, down_adapter_second=down_adapter_second)


adapter_scale = 2.0
highest_precision = lax.Precision.HIGHEST


def wide_dot(left, right):
    return jnp.dot(left.astype(jnp.float32), right.astype(jnp.float32), precision=highest_precision)


def into_hidden(row_block, tile_values, slot_index, pattern):
    row_count = row_block.shape[0]
    block_step = tile_values.shape[-1]
    split_rows = row_block.reshape(row_count, WB_DEV, block_step)
    picked = jnp.take(split_rows, slot_index % WB_DEV, axis=1).astype(jnp.float32)
    product = jnp.einsum(pattern, picked, tile_values.astype(jnp.float32), precision=highest_precision)
    onehot = (slot_index[:, None] // WB_DEV == jnp.arange(HB_DEV)[None, :]).astype(jnp.float32)
    merged = jnp.einsum('rkj,kh->rhj', product, onehot, precision=highest_precision)
    return merged.reshape(row_count, HB_DEV * block_step)


def into_width(row_block, tile_values, slot_index):
    row_count = row_block.shape[0]
    block_step = tile_values.shape[-1]
    split_rows = row_block.reshape(row_count, HB_DEV, block_step)
    which_hidden = jnp.minimum(slot_index // WB_DEV, HB_DEV - 1)
    picked = jnp.take(split_rows, which_hidden, axis=1).astype(jnp.float32)
    product = jnp.einsum('rkj,kcj->rkc', picked, tile_values.astype(jnp.float32), precision=highest_precision)
    live_slot = slot_index < HB_DEV * WB_DEV
    onehot = (((slot_index % WB_DEV)[:, None] == jnp.arange(WB_DEV)[None, :]) & live_slot[:, None]).astype(jnp.float32)
    merged = jnp.einsum('rkc,kw->rwc', product, onehot, precision=highest_precision)
    return merged.reshape(row_count, WB_DEV * block_step)


def whole_hidden(tile_grid, slot_grid, split_rows, pattern):
    row_count = split_rows.shape[1]

    def one_hidden(pair):
        parts = jax.vmap(lambda values, index, rows_here: into_hidden(rows_here, values, index, pattern))(pair[0], pair[1], split_rows)
        return jnp.sum(parts, axis=0)

    stacked = lax.map(one_hidden, (tile_grid, slot_grid))
    return stacked.transpose(1, 0, 2).reshape(row_count, HIDDEN_UNITS)


def reference(tokens, output_gradient, gate_weight_blocks, gate_block_places, up_weight_blocks, up_block_places, down_weight_blocks, down_block_places, gate_adapter_first, gate_adapter_second, up_adapter_first, up_adapter_second, down_adapter_first, down_adapter_second):
    row_count = tokens.shape[0]
    tok_split = tokens.reshape(row_count, N_WID, WB_DEV * BLOCK).transpose(1, 0, 2)
    grad_split = output_gradient.reshape(row_count, N_WID, WB_DEV * BLOCK).transpose(1, 0, 2)
    gate_piece = whole_hidden(gate_weight_blocks, gate_block_places, tok_split, 'rkc,kcj->rkj')
    up_piece = whole_hidden(up_weight_blocks, up_block_places, tok_split, 'rkc,kcj->rkj')
    down_piece = whole_hidden(down_weight_blocks, down_block_places, grad_split, 'rkc,kjc->rkj')
    gate_rank_rows = wide_dot(tokens, gate_adapter_first)
    up_rank_rows = wide_dot(tokens, up_adapter_first)
    rank_gradient = wide_dot(output_gradient, down_adapter_second.T)
    gate_activation = gate_piece + adapter_scale * wide_dot(gate_rank_rows, gate_adapter_second)
    up_activation = up_piece + adapter_scale * wide_dot(up_rank_rows, up_adapter_second)
    hidden_gradient = down_piece + adapter_scale * wide_dot(rank_gradient, down_adapter_first.T)
    sigmoid_gate = jax.nn.sigmoid(gate_activation)
    activated = gate_activation * sigmoid_gate
    hidden_state = (activated * up_activation).astype(jnp.bfloat16)
    gate_gradient = (hidden_gradient * up_activation * sigmoid_gate * (1.0 + gate_activation * (1.0 - sigmoid_gate))).astype(jnp.bfloat16)
    up_gradient = (hidden_gradient * activated).astype(jnp.bfloat16)
    gate_backward = wide_dot(gate_gradient, gate_adapter_second.T)
    up_backward = wide_dot(up_gradient, up_adapter_second.T)
    gate_split = gate_gradient.reshape(row_count, N_HID, HB_DEV * BLOCK).transpose(1, 0, 2)
    up_split = up_gradient.reshape(row_count, N_HID, HB_DEV * BLOCK).transpose(1, 0, 2)

    def add_tile(running_total, item):
        gate_vals, gate_index, up_vals, up_index, gate_rows, up_rows = item
        per_wid = jax.vmap(lambda gv, gi, uv, ui: into_width(gate_rows, gv, gi) + into_width(up_rows, uv, ui))(gate_vals, gate_index, up_vals, up_index)
        return running_total + per_wid.transpose(1, 0, 2).reshape(row_count, MODEL_WIDTH), None

    start_total = jnp.zeros((row_count, MODEL_WIDTH), jnp.float32)
    running_total, unused = lax.scan(add_tile, start_total, (gate_weight_blocks, gate_block_places, up_weight_blocks, up_block_places, gate_split, up_split))
    rank_product = wide_dot(gate_backward, gate_adapter_first.T) + wide_dot(up_backward, up_adapter_first.T)
    token_gradient = (running_total + adapter_scale * rank_product).astype(jnp.bfloat16)
    gate_adapter_gradient = adapter_scale * wide_dot(gate_rank_rows.T, gate_gradient)
    up_adapter_gradient = adapter_scale * wide_dot(up_rank_rows.T, up_gradient)
    down_rank_rows = wide_dot(hidden_state, down_adapter_first)
    down_adapter_gradient = adapter_scale * wide_dot(down_rank_rows.T, output_gradient)
    return (token_gradient, gate_adapter_gradient, up_adapter_gradient, down_adapter_gradient)
```

```python
import functools

import jax
import jax.numpy as jnp
from jax import lax
from jax.experimental import pallas as pl
from jax.experimental.pallas import tpu as pltpu
from jax.sharding import PartitionSpec as P

adapter_scale = 2.0
MESH = pl.DeviceIdType.MESH
bf16, f32 = jnp.bfloat16, jnp.float32


def dot(left, right):
    return jnp.dot(left, right, preferred_element_type=f32)


def dot_nt(left, right):
    return lax.dot_general(left, right, (((1,), (1,)), ((), ())), preferred_element_type=f32)


def two_parts(value):
    high = value.astype(bf16)
    low = (value - high.astype(f32)).astype(bf16)
    return jnp.concatenate([high, low], axis=0)


def wide(product):
    half = product.shape[0] // 2
    return product[:half] + product[half:]


def kernel(
    n_hid, n_wid, n_dat,
    tok, dy, wg, wu, wd, pg, pu, pd, ag, bg, au, bu, ad, bd,
    tok_out, gate_out, up_out, down_out,
    slots, inv_v, inv_s, wcat, wdn, bcat, a_first, a2, ad_v, bd_v,
    xg, yg, x_v, y_v, fbuf, rbuf, hbuf, sbuf, tbuf, dbuf, gbuf, ebuf, acc,
    local_sem, x_s, x_r, y_s, y_r, f_s, f_r, r_s, r_r, h_s, h_r, t_s, t_r, d_s, d_r, g_s, g_r, e_s, e_r,
):
    me_h, me_w, me_d = lax.axis_index("hid"), lax.axis_index("wid"), lax.axis_index("dat")
    own, width = tok.shape
    rows = own * n_hid
    cap, step = wg.shape[2], wg.shape[3]
    hid = bg.shape[1]
    rank = bg.shape[0]
    hb, wb = hid // step, width // step

    def peers(me, n):
        return [lax.rem(me + d, n) for d in range(1, n)]

    groups = (("hid", me_h, n_hid), ("wid", me_w, n_wid), ("dat", me_d, n_dat))
    barrier = pltpu.get_barrier_semaphore()
    for axis, me, n in groups:
        for peer in peers(me, n):
            pl.semaphore_signal(barrier, inc=1, device_id={axis: peer}, device_id_type=MESH)

    pairs = [
        (tok, xg.at[me_h]),
        (dy, yg.at[me_h]),
        (wg.at[0, 0], slots.at[0, pl.ds(0, cap)]),
        (wu.at[0, 0], slots.at[1, pl.ds(0, cap)]),
        (wd.at[0, 0], slots.at[2, pl.ds(0, cap)]),
        (ag, a_first.at[0]),
        (au, a_first.at[1]),
        (bg, bcat.at[pl.ds(0, rank), pl.ds(0, hid)]),
        (bu, bcat.at[pl.ds(rank, rank), pl.ds(hid, hid)]),
        (ad, ad_v),
        (bd, bd_v),
    ]
    local = [pltpu.make_async_copy(s, d, local_sem.at[i]) for i, (s, d) in enumerate(pairs)]
    for copy in local:
        copy.start()

    pl.semaphore_wait(barrier, n_hid + n_wid + n_dat - 3)

    def send(source, buf, axis, me, n, send_sem, recv_sem):
        copies = []
        for d, peer in enumerate(peers(me, n)):
            copy = pltpu.make_async_remote_copy(
                src_ref=source(peer), dst_ref=buf.at[me],
                send_sem=send_sem.at[d], recv_sem=recv_sem.at[me],
                device_id={axis: peer}, device_id_type=MESH,
            )
            copy.start()
            copies.append(copy)
        return copies

    def arrive(buf, axis, me, n, send_sem, recv_sem):
        for d, peer in enumerate(peers(me, n)):
            pltpu.make_async_remote_copy(
                src_ref=buf.at[peer], dst_ref=buf.at[peer],
                send_sem=send_sem.at[d], recv_sem=recv_sem.at[peer],
                device_id={axis: peer}, device_id_type=MESH,
            ).wait_recv()

    hid_axis, wid_axis, dat_axis = groups
    sent = send(lambda peer: tok, xg, *hid_axis, x_s, x_r)
    sent += send(lambda peer: dy, yg, *hid_axis, y_s, y_r)

    lanes = inv_v.shape[1]
    lane = lax.broadcasted_iota(jnp.int32, (8, lanes), 1)
    row = lax.broadcasted_iota(jnp.int32, (8, lanes), 0)
    inverse = jnp.full((8, lanes), cap, jnp.int32)
    for m, places in enumerate((pg, pu, pd)):
        mine = jnp.where(row == m, lane, -1)
        for k in range(cap):
            inverse = jnp.where(mine == places[0, 0, k], k, inverse)
    inv_v[...] = inverse
    inv_copy = pltpu.make_async_copy(inv_v, inv_s, local_sem.at[len(pairs)])
    inv_copy.start()
    for m in range(3):
        slots[m, cap] = jnp.zeros((step, step), bf16)
    bcat[:rank, hid:] = jnp.zeros((rank, hid), bf16)
    bcat[rank:, :hid] = jnp.zeros((rank, hid), bf16)
    for copy in local[5:]:
        copy.wait()
    a2[:, :rank] = a_first[0]
    a2[:, rank:] = a_first[1]
    inv_copy.wait()
    for copy in local[2:5]:
        copy.wait()

    def lay(w, carry):
        start = pl.multiple_of(w * step, step)
        for h in range(hb):
            for m in range(2):
                wcat[pl.ds(start, step), m * hid + h * step : m * hid + (h + 1) * step] = slots[
                    m, inv_s[m, h * wb + w]
                ]
            wdn[h * step : (h + 1) * step, pl.ds(start, step)] = slots[2, inv_s[2, h * wb + w]]
        return carry

    lax.fori_loop(0, wb, lay, 0)

    def assemble(gathered, whole):
        parts = [gathered[i].astype(f32) for i in range(n_hid)]
        whole[...] = jnp.concatenate(parts, axis=0).astype(bf16)

    local[0].wait()
    arrive(xg, *hid_axis, x_s, x_r)
    assemble(xg, x_v)
    ranks = dot(x_v[...], a2[...])
    rbuf[me_w] = ranks
    low_rank = wide(dot(two_parts(ranks), bcat[...]))
    fbuf[me_w] = (dot(x_v[...], wcat[...]) + adapter_scale * low_rank).astype(bf16)
    sent += send(lambda peer: fbuf.at[me_w], fbuf, *wid_axis, f_s, f_r)
    sent += send(lambda peer: rbuf.at[me_w], rbuf, *wid_axis, r_s, r_r)

    local[1].wait()
    arrive(yg, *hid_axis, y_s, y_r)
    assemble(yg, y_v)
    grad_rank = dot_nt(y_v[...], bd_v[...])
    back_low = wide(dot_nt(two_parts(grad_rank), ad_v[...]))
    hbuf[me_w] = (dot_nt(y_v[...], wdn[...]) + adapter_scale * back_low).astype(bf16)
    sent += send(lambda peer: hbuf.at[me_w], hbuf, *wid_axis, h_s, h_r)

    arrive(fbuf, *wid_axis, f_s, f_r)
    arrive(rbuf, *wid_axis, r_s, r_r)
    both = sum(fbuf[i].astype(f32) for i in range(n_wid))
    ranks = sum(rbuf[i] for i in range(n_wid))
    gate, up = both[:, :hid], both[:, hid:]
    sig = jax.nn.sigmoid(gate)
    act = gate * sig
    hidden = (act * up).astype(bf16)
    dbuf[me_h] = dot(hidden, ad_v[...])
    sent += send(lambda peer: dbuf.at[me_h], dbuf, *hid_axis, d_s, d_r)
    slope = up * sig * (1.0 + gate * (1.0 - sig))
    arrive(hbuf, *wid_axis, h_s, h_r)
    hidden_grad = sum(hbuf[i].astype(f32) for i in range(n_wid))
    grads = jnp.concatenate(
        [(hidden_grad * slope).astype(bf16), (hidden_grad * act).astype(bf16)], axis=1
    )
    backs = two_parts(adapter_scale * dot_nt(grads, bcat[...]))
    total = dot_nt(grads, wcat[...]) + wide(dot_nt(backs, a2[...]))
    for i in range(n_hid):
        sbuf[i] = total[i * own : (i + 1) * own].astype(bf16)
    acc[...] = total.reshape(n_hid, own, width)
    sent += send(lambda peer: sbuf.at[peer], tbuf, *hid_axis, t_s, t_r)

    ranks_t = adapter_scale * ranks.T
    gbuf[me_d, :, :hid] = wide(dot(two_parts(ranks_t[:rank]), grads[:, :hid]))
    gbuf[me_d, :, hid:] = wide(dot(two_parts(ranks_t[rank:]), grads[:, hid:]))
    sent += send(lambda peer: gbuf.at[me_d], gbuf, *dat_axis, g_s, g_r)

    arrive(dbuf, *hid_axis, d_s, d_r)
    down_rank = adapter_scale * sum(dbuf[i] for i in range(n_hid)).T
    ebuf[me_d] = wide(dot(two_parts(down_rank), y_v[...]))
    sent += send(lambda peer: ebuf.at[me_d], ebuf, *dat_axis, e_s, e_r)

    arrive(gbuf, *dat_axis, g_s, g_r)
    summed = sum(gbuf[i] for i in range(n_dat))
    gate_out[...] = summed[:, :hid]
    up_out[...] = summed[:, hid:]
    arrive(tbuf, *hid_axis, t_s, t_r)
    mine = acc[me_h]
    for peer in peers(me_h, n_hid):
        mine = mine + tbuf[peer].astype(f32)
    tok_out[...] = mine.astype(bf16)
    arrive(ebuf, *dat_axis, e_s, e_r)
    down_out[...] = sum(ebuf[i] for i in range(n_dat))
    for copy in sent:
        copy.wait_send()


def shards(
    n_hid, n_wid, n_dat,
    tokens, output_gradient,
    gate_weight_blocks, gate_block_places,
    up_weight_blocks, up_block_places,
    down_weight_blocks, down_block_places,
    gate_adapter_first, gate_adapter_second,
    up_adapter_first, up_adapter_second,
    down_adapter_first, down_adapter_second,
):
    own, width = tokens.shape
    rows = own * n_hid
    cap, step = gate_weight_blocks.shape[2], gate_weight_blocks.shape[3]
    rank, hid = gate_adapter_second.shape
    positions = (hid // step) * (width // step)
    lanes = -(-positions // 128) * 128
    any_spec = pl.BlockSpec(memory_space=pl.ANY)
    smem_spec = pl.BlockSpec(memory_space=pltpu.SMEM)
    vmem_spec = pl.BlockSpec(memory_space=pltpu.VMEM)
    V = pltpu.VMEM
    D = pltpu.SemaphoreType.DMA

    def sems(n):
        return [D((max(n - 1, 1),)), D((n,))]

    return pl.pallas_call(
        functools.partial(kernel, n_hid, n_wid, n_dat),
        out_shape=(
            jax.ShapeDtypeStruct((own, width), bf16),
            jax.ShapeDtypeStruct((rank, hid), f32),
            jax.ShapeDtypeStruct((rank, hid), f32),
            jax.ShapeDtypeStruct((rank, width), f32),
        ),
        in_specs=[any_spec] * 5 + [smem_spec] * 3 + [any_spec] * 6,
        out_specs=(vmem_spec,) * 4,
        scratch_shapes=[
            V((3, cap + 1, step, step), bf16),
            V((8, lanes), jnp.int32),
            pltpu.SMEM((8, lanes), jnp.int32),
            V((width, 2 * hid), bf16),
            V((hid, width), bf16),
            V((2 * rank, 2 * hid), bf16),
            V((2, width, rank), bf16),
            V((width, 2 * rank), bf16),
            V((hid, rank), bf16),
            V((rank, width), bf16),
            V((n_hid, own, width), bf16),
            V((n_hid, own, width), bf16),
            V((rows, width), bf16),
            V((rows, width), bf16),
            V((n_wid, rows, 2 * hid), bf16),
            V((n_wid, rows, 2 * rank), f32),
            V((n_wid, rows, hid), bf16),
            V((n_hid, own, width), bf16),
            V((n_hid, own, width), bf16),
            V((n_hid, rows, rank), f32),
            V((n_dat, rank, 2 * hid), f32),
            V((n_dat, rank, width), f32),
            V((n_hid, own, width), f32),
            D((12,)),
            *sems(n_hid), *sems(n_hid), *sems(n_wid), *sems(n_wid), *sems(n_wid),
            *sems(n_hid), *sems(n_hid), *sems(n_dat), *sems(n_dat),
        ],
        compiler_params=pltpu.CompilerParams(
            collective_id=0, has_side_effects=True, vmem_limit_bytes=56 * 1024 * 1024
        ),
    )(
        tokens, output_gradient,
        gate_weight_blocks, up_weight_blocks, down_weight_blocks,
        gate_block_places, up_block_places, down_block_places,
        gate_adapter_first, gate_adapter_second,
        up_adapter_first, up_adapter_second,
        down_adapter_first, down_adapter_second,
    )


def solution(mesh):
    sizes = (mesh.shape["hid"], mesh.shape["wid"], mesh.shape["dat"])
    return jax.shard_map(
        functools.partial(shards, *sizes),
        mesh=mesh,
        in_specs=(
            P(("grp", "hid", "dat"), "wid"),
            P(("grp", "hid", "dat"), "wid"),
            P("hid", "wid", None, None, None),
            P("hid", "wid", None),
            P("hid", "wid", None, None, None),
            P("hid", "wid", None),
            P("hid", "wid", None, None, None),
            P("hid", "wid", None),
            P("wid", None),
            P(None, "hid"),
            P("wid", None),
            P(None, "hid"),
            P("hid", None),
            P(None, "wid"),
        ),
        out_specs=(
            P(("grp", "hid", "dat"), "wid"),
            P("grp", "hid"),
            P("grp", "hid"),
            P("grp", "wid"),
        ),
        check_vma=False,
    )
```

```python
import functools

import jax
import jax.numpy as jnp
from jax import lax
from jax.experimental import pallas as pl
from jax.experimental.pallas import tpu as pltpu
from jax.sharding import PartitionSpec as P

adapter_scale = 2.0
MESH = pl.DeviceIdType.MESH
bf16, f32 = jnp.bfloat16, jnp.float32


def dot(left, right):
    return jnp.dot(left, right, preferred_element_type=f32)


def dot_nt(left, right):
    return lax.dot_general(left, right, (((1,), (1,)), ((), ())), preferred_element_type=f32)


def two_parts(value):
    high = value.astype(bf16)
    low = (value - high.astype(f32)).astype(bf16)
    return jnp.concatenate([high, low], axis=0)


def wide(product):
    half = product.shape[0] // 2
    return product[:half] + product[half:]


def kernel(
    n_hid, n_wid, n_dat,
    tok, dy, wg, wu, wd, pg, pu, pd, ag, bg, au, bu, ad, bd,
    tok_out, gate_out, up_out, down_out,
    slots, places, inv_v, inv_s, wcat, wdn, bcat, a2, ad_v, bd_v,
    xg, yg, x_v, y_v, fbuf, rbuf, hbuf, sbuf, tbuf, dbuf, gbuf, ebuf, acc,
    local_sem, x_s, x_r, y_s, y_r, f_s, f_r, r_s, r_r, h_s, h_r, t_s, t_r, d_s, d_r, g_s, g_r, e_s, e_r,
):
    me_h, me_w, me_d = lax.axis_index("hid"), lax.axis_index("wid"), lax.axis_index("dat")
    own, width = tok.shape
    rows = own * n_hid
    cap, step = wg.shape[2], wg.shape[3]
    hid = bg.shape[1]
    rank = bg.shape[0]
    hb, wb = hid // step, width // step

    def peers(me, n):
        return [lax.rem(me + d, n) for d in range(1, n)]

    groups = (("hid", me_h, n_hid), ("wid", me_w, n_wid), ("dat", me_d, n_dat))
    barrier = pltpu.get_barrier_semaphore()
    for axis, me, n in groups:
        for peer in peers(me, n):
            pl.semaphore_signal(barrier, inc=1, device_id={axis: peer}, device_id_type=MESH)

    pairs = [
        (tok, xg.at[me_h]),
        (dy, yg.at[me_h]),
        (wg.at[0, 0], slots.at[0, pl.ds(0, cap)]),
        (wu.at[0, 0], slots.at[1, pl.ds(0, cap)]),
        (wd.at[0, 0], slots.at[2, pl.ds(0, cap)]),
        (ag, a2.at[pl.ds(0, rank)]),
        (au, a2.at[pl.ds(rank, rank)]),
        (bg, bcat.at[pl.ds(0, rank), pl.ds(0, hid)]),
        (bu, bcat.at[pl.ds(rank, rank), pl.ds(hid, hid)]),
        (ad, ad_v),
        (bd, bd_v),
        (pg.at[0], places.at[0]),
        (pu.at[0], places.at[1]),
        (pd.at[0], places.at[2]),
    ]
    local = [pltpu.make_async_copy(s, d, local_sem.at[i]) for i, (s, d) in enumerate(pairs)]
    for copy in local:
        copy.start()

    pl.semaphore_wait(barrier, n_hid + n_wid + n_dat - 3)

    def send(source, buf, axis, me, n, send_sem, recv_sem):
        copies = []
        for d, peer in enumerate(peers(me, n)):
            copy = pltpu.make_async_remote_copy(
                src_ref=source(peer), dst_ref=buf.at[me],
                send_sem=send_sem.at[d], recv_sem=recv_sem.at[me],
                device_id={axis: peer}, device_id_type=MESH,
            )
            copy.start()
            copies.append(copy)
        return copies

    def arrive(buf, axis, me, n, send_sem, recv_sem):
        for d, peer in enumerate(peers(me, n)):
            pltpu.make_async_remote_copy(
                src_ref=buf.at[peer], dst_ref=buf.at[peer],
                send_sem=send_sem.at[d], recv_sem=recv_sem.at[peer],
                device_id={axis: peer}, device_id_type=MESH,
            ).wait_recv()

    hid_axis, wid_axis, dat_axis = groups
    sent = send(lambda peer: tok, xg, *hid_axis, x_s, x_r)
    sent += send(lambda peer: dy, yg, *hid_axis, y_s, y_r)

    lanes = inv_v.shape[1]
    lane = lax.broadcasted_iota(jnp.int32, (8, lanes), 1)
    row = lax.broadcasted_iota(jnp.int32, (8, lanes), 0)
    inverse = jnp.full((8, lanes), cap, jnp.int32)
    for m in range(3):
        local[11 + m].wait()
        mine = jnp.where(row == m, lane, -1)
        for k in range(cap):
            inverse = jnp.where(mine == places[m, 0, k], k, inverse)
    inv_v[...] = inverse
    inv_copy = pltpu.make_async_copy(inv_v, inv_s, local_sem.at[len(pairs)])
    inv_copy.start()
    for m in range(3):
        slots[m, cap] = jnp.zeros((step, step), bf16)
    bcat[:rank, hid:] = jnp.zeros((rank, hid), bf16)
    bcat[rank:, :hid] = jnp.zeros((rank, hid), bf16)
    for copy in local[5:11]:
        copy.wait()
    inv_copy.wait()
    for copy in local[2:5]:
        copy.wait()

    def lay(w, carry):
        start = pl.multiple_of(w * step, step)
        for h in range(hb):
            for m in range(2):
                wcat[pl.ds(start, step), m * hid + h * step : m * hid + (h + 1) * step] = slots[
                    m, inv_s[m, h * wb + w]
                ]
            wdn[h * step : (h + 1) * step, pl.ds(start, step)] = slots[2, inv_s[2, h * wb + w]]
        return carry

    lax.fori_loop(0, wb, lay, 0)

    def assemble(gathered, whole):
        parts = [gathered[i].astype(f32) for i in range(n_hid)]
        whole[...] = jnp.concatenate(parts, axis=0).astype(bf16)

    local[0].wait()
    arrive(xg, *hid_axis, x_s, x_r)
    assemble(xg, x_v)
    ranks = dot_nt(x_v[...], a2[...])
    rbuf[me_w] = ranks
    low_rank = wide(dot(two_parts(ranks), bcat[...]))
    fbuf[me_w] = dot(x_v[...], wcat[...]) + adapter_scale * low_rank
    sent += send(lambda peer: fbuf.at[me_w], fbuf, *wid_axis, f_s, f_r)
    sent += send(lambda peer: rbuf.at[me_w], rbuf, *wid_axis, r_s, r_r)

    local[1].wait()
    arrive(yg, *hid_axis, y_s, y_r)
    assemble(yg, y_v)
    grad_rank = dot_nt(y_v[...], bd_v[...])
    back_low = wide(dot(two_parts(grad_rank), ad_v[...]))
    hbuf[me_w] = (dot_nt(y_v[...], wdn[...]) + adapter_scale * back_low).astype(bf16)
    sent += send(lambda peer: hbuf.at[me_w], hbuf, *wid_axis, h_s, h_r)

    arrive(fbuf, *wid_axis, f_s, f_r)
    arrive(rbuf, *wid_axis, r_s, r_r)
    both = sum(fbuf[i] for i in range(n_wid))
    ranks = sum(rbuf[i] for i in range(n_wid))
    gate, up = both[:, :hid], both[:, hid:]
    sig = jax.nn.sigmoid(gate)
    act = gate * sig
    hidden = (act * up).astype(bf16)
    dbuf[me_h] = dot_nt(hidden, ad_v[...])
    sent += send(lambda peer: dbuf.at[me_h], dbuf, *hid_axis, d_s, d_r)
    slope = up * sig * (1.0 + gate * (1.0 - sig))
    arrive(hbuf, *wid_axis, h_s, h_r)
    hidden_grad = sum(hbuf[i].astype(f32) for i in range(n_wid))
    grads = jnp.concatenate(
        [(hidden_grad * slope).astype(bf16), (hidden_grad * act).astype(bf16)], axis=1
    )
    backs = two_parts(adapter_scale * dot_nt(grads, bcat[...]))
    total = dot_nt(grads, wcat[...]) + wide(dot(backs, a2[...]))
    for i in range(n_hid):
        sbuf[i] = total[i * own : (i + 1) * own].astype(bf16)
    acc[...] = total.reshape(n_hid, own, width)
    sent += send(lambda peer: sbuf.at[peer], tbuf, *hid_axis, t_s, t_r)

    ranks_t = adapter_scale * ranks.T
    gbuf[me_d, :, :hid] = wide(dot(two_parts(ranks_t[:rank]), grads[:, :hid]))
    gbuf[me_d, :, hid:] = wide(dot(two_parts(ranks_t[rank:]), grads[:, hid:]))
    sent += send(lambda peer: gbuf.at[me_d], gbuf, *dat_axis, g_s, g_r)

    arrive(dbuf, *hid_axis, d_s, d_r)
    down_rank = adapter_scale * sum(dbuf[i] for i in range(n_hid)).T
    ebuf[me_d] = wide(dot(two_parts(down_rank), y_v[...]))
    sent += send(lambda peer: ebuf.at[me_d], ebuf, *dat_axis, e_s, e_r)

    arrive(gbuf, *dat_axis, g_s, g_r)
    summed = sum(gbuf[i] for i in range(n_dat))
    gate_out[...] = summed[:, :hid]
    up_out[...] = summed[:, hid:]
    arrive(tbuf, *hid_axis, t_s, t_r)
    mine = acc[me_h]
    for peer in peers(me_h, n_hid):
        mine = mine + tbuf[peer].astype(f32)
    tok_out[...] = mine.astype(bf16)
    arrive(ebuf, *dat_axis, e_s, e_r)
    down_out[...] = sum(ebuf[i] for i in range(n_dat))
    for copy in sent:
        copy.wait_send()


def hand_out(*refs):
    sems = refs[8]
    copies = [pltpu.make_async_copy(refs[i], refs[i + 4], sems.at[i]) for i in range(4)]
    for copy in copies:
        copy.start()
    for copy in copies:
        copy.wait()


def shards(
    n_hid, n_wid, n_dat,
    tokens, output_gradient,
    gate_weight_blocks, gate_block_places,
    up_weight_blocks, up_block_places,
    down_weight_blocks, down_block_places,
    gate_adapter_first, gate_adapter_second,
    up_adapter_first, up_adapter_second,
    down_adapter_first, down_adapter_second,
):
    own, width = tokens.shape
    rows = own * n_hid
    cap, step = gate_weight_blocks.shape[2], gate_weight_blocks.shape[3]
    rank, hid = gate_adapter_second.shape
    positions = (hid // step) * (width // step)
    lanes = -(-positions // 128) * 128
    any_spec = pl.BlockSpec(memory_space=pl.ANY)
    vmem_spec = pl.BlockSpec(memory_space=pltpu.VMEM)
    V = pltpu.VMEM
    D = pltpu.SemaphoreType.DMA

    shapes = (
        jax.ShapeDtypeStruct((own, width), bf16),
        jax.ShapeDtypeStruct((rank, hid), f32),
        jax.ShapeDtypeStruct((rank, hid), f32),
        jax.ShapeDtypeStruct((rank, width), f32),
    )

    def sems(n):
        return [D((max(n - 1, 1),)), D((n,))]

    results = pl.pallas_call(
        functools.partial(kernel, n_hid, n_wid, n_dat),
        out_shape=shapes,
        in_specs=[any_spec] * 14,
        out_specs=(vmem_spec,) * 4,
        scratch_shapes=[
            V((3, cap + 1, step, step), bf16),
            pltpu.SMEM((3, 1, cap), jnp.int32),
            V((8, lanes), jnp.int32),
            pltpu.SMEM((8, lanes), jnp.int32),
            V((width, 2 * hid), bf16),
            V((hid, width), bf16),
            V((2 * rank, 2 * hid), bf16),
            V((2 * rank, width), bf16),
            V((rank, hid), bf16),
            V((rank, width), bf16),
            V((n_hid, own, width), bf16),
            V((n_hid, own, width), bf16),
            V((rows, width), bf16),
            V((rows, width), bf16),
            V((n_wid, rows, 2 * hid), f32),
            V((n_wid, rows, 2 * rank), f32),
            V((n_wid, rows, hid), bf16),
            V((n_hid, own, width), bf16),
            V((n_hid, own, width), bf16),
            V((n_hid, rows, rank), f32),
            V((n_dat, rank, 2 * hid), f32),
            V((n_dat, rank, width), f32),
            V((n_hid, own, width), f32),
            D((15,)),
            *sems(n_hid), *sems(n_hid), *sems(n_wid), *sems(n_wid), *sems(n_wid),
            *sems(n_hid), *sems(n_hid), *sems(n_dat), *sems(n_dat),
        ],
        compiler_params=pltpu.CompilerParams(
            collective_id=0, has_side_effects=True, vmem_limit_bytes=40 * 1024 * 1024
        ),
    )(
        *(
            pltpu.with_memory_space_constraint(operand, pltpu.HBM)
            for operand in (
                tokens, output_gradient,
                gate_weight_blocks, up_weight_blocks, down_weight_blocks,
                gate_block_places, up_block_places, down_block_places,
                gate_adapter_first.T, gate_adapter_second,
                up_adapter_first.T, up_adapter_second,
                down_adapter_first.T, down_adapter_second,
            )
        ),
    )
    return pl.pallas_call(
        hand_out,
        out_shape=shapes,
        in_specs=[any_spec] * 4,
        out_specs=(any_spec,) * 4,
        scratch_shapes=[D((4,))],
    )(*results)


def solution(mesh):
    sizes = (mesh.shape["hid"], mesh.shape["wid"], mesh.shape["dat"])
    return jax.shard_map(
        functools.partial(shards, *sizes),
        mesh=mesh,
        in_specs=(
            P(("grp", "hid", "dat"), "wid"),
            P(("grp", "hid", "dat"), "wid"),
            P("hid", "wid", None, None, None),
            P("hid", "wid", None),
            P("hid", "wid", None, None, None),
            P("hid", "wid", None),
            P("hid", "wid", None, None, None),
            P("hid", "wid", None),
            P("wid", None),
            P(None, "hid"),
            P("wid", None),
            P(None, "hid"),
            P("hid", None),
            P(None, "wid"),
        ),
        out_specs=(
            P(("grp", "hid", "dat"), "wid"),
            P("grp", "hid"),
            P("grp", "hid"),
            P("grp", "wid"),
        ),
        check_vma=False,
    )
```

```python
import functools

import jax
import jax.numpy as jnp
from jax import lax
from jax.experimental import pallas as pl
from jax.experimental.pallas import tpu as pltpu
from jax.sharding import PartitionSpec as P

adapter_scale = 2.0
MESH = pl.DeviceIdType.MESH
bf16, f32 = jnp.bfloat16, jnp.float32


def dot(left, right):
    return jnp.dot(left, right, preferred_element_type=f32)


def dot_nt(left, right):
    return lax.dot_general(left, right, (((1,), (1,)), ((), ())), preferred_element_type=f32)


def two_parts(value):
    high = value.astype(bf16)
    low = (value - high.astype(f32)).astype(bf16)
    return jnp.concatenate([high, low], axis=0)


def wide(product):
    half = product.shape[0] // 2
    return product[:half] + product[half:]


def kernel(
    n_hid, n_wid, n_dat,
    tok, dy, wg, wu, wd, pg, pu, pd, ag, bg, au, bu, ad, bd,
    tok_out, gate_out, up_out, down_out,
    slots, places, inv_v, inv_s, wcat, wdn, bcat, a2, ad_v, bd_v,
    xg, yg, x_v, y_v, fbuf, rbuf, hbuf, sbuf, tbuf, dbuf, gbuf, ebuf, acc,
    local_sem, x_s, x_r, y_s, y_r, f_s, f_r, r_s, r_r, h_s, h_r, t_s, t_r, d_s, d_r, g_s, g_r, e_s, e_r,
):
    me_h, me_w, me_d = lax.axis_index("hid"), lax.axis_index("wid"), lax.axis_index("dat")
    own, width = tok.shape
    rows = own * n_hid
    cap, step = wg.shape[2], wg.shape[3]
    hid = bg.shape[1]
    rank = bg.shape[0]
    hb, wb = hid // step, width // step

    def peers(me, n):
        return [lax.rem(me + d, n) for d in range(1, n)]

    groups = (("hid", me_h, n_hid), ("wid", me_w, n_wid), ("dat", me_d, n_dat))
    barrier = pltpu.get_barrier_semaphore()
    for axis, me, n in groups:
        for peer in peers(me, n):
            pl.semaphore_signal(barrier, inc=1, device_id={axis: peer}, device_id_type=MESH)

    pairs = [
        (tok, xg.at[me_h]),
        (dy, yg.at[me_h]),
        (wg.at[0, 0], slots.at[0, pl.ds(0, cap)]),
        (wu.at[0, 0], slots.at[1, pl.ds(0, cap)]),
        (wd.at[0, 0], slots.at[2, pl.ds(0, cap)]),
        (ag, a2.at[pl.ds(0, rank)]),
        (au, a2.at[pl.ds(rank, rank)]),
        (bg, bcat.at[pl.ds(0, rank), pl.ds(0, hid)]),
        (bu, bcat.at[pl.ds(rank, rank), pl.ds(hid, hid)]),
        (ad, ad_v),
        (bd, bd_v),
        (pg.at[0], places.at[0]),
        (pu.at[0], places.at[1]),
        (pd.at[0], places.at[2]),
    ]
    local = [pltpu.make_async_copy(s, d, local_sem.at[i]) for i, (s, d) in enumerate(pairs)]
    for copy in local:
        copy.start()

    pl.semaphore_wait(barrier, n_hid + n_wid + n_dat - 3)

    def send(source, buf, axis, me, n, send_sem, recv_sem):
        copies = []
        for d, peer in enumerate(peers(me, n)):
            copy = pltpu.make_async_remote_copy(
                src_ref=source(peer), dst_ref=buf.at[me],
                send_sem=send_sem.at[d], recv_sem=recv_sem.at[me],
                device_id={axis: peer}, device_id_type=MESH,
            )
            copy.start()
            copies.append(copy)
        return copies

    def arrive(buf, axis, me, n, send_sem, recv_sem):
        for d, peer in enumerate(peers(me, n)):
            pltpu.make_async_remote_copy(
                src_ref=buf.at[peer], dst_ref=buf.at[peer],
                send_sem=send_sem.at[d], recv_sem=recv_sem.at[peer],
                device_id={axis: peer}, device_id_type=MESH,
            ).wait_recv()

    hid_axis, wid_axis, dat_axis = groups
    sent = send(lambda peer: tok, xg, *hid_axis, x_s, x_r)
    sent += send(lambda peer: dy, yg, *hid_axis, y_s, y_r)

    lanes = inv_v.shape[1]
    lane = lax.broadcasted_iota(jnp.int32, (8, lanes), 1)
    row = lax.broadcasted_iota(jnp.int32, (8, lanes), 0)
    inverse = jnp.full((8, lanes), cap, jnp.int32)
    for m in range(3):
        local[11 + m].wait()
        mine = jnp.where(row == m, lane, -1)
        for k in range(cap):
            inverse = jnp.where(mine == places[m, 0, k], k, inverse)
    inv_v[...] = inverse
    inv_copy = pltpu.make_async_copy(inv_v, inv_s, local_sem.at[len(pairs)])
    inv_copy.start()
    for m in range(3):
        slots[m, cap] = jnp.zeros((step, step), bf16)
    bcat[:rank, hid:] = jnp.zeros((rank, hid), bf16)
    bcat[rank:, :hid] = jnp.zeros((rank, hid), bf16)
    for copy in local[5:11]:
        copy.wait()
    inv_copy.wait()
    for copy in local[2:5]:
        copy.wait()

    def lay(w, carry):
        start = pl.multiple_of(w * step, step)
        for h in range(hb):
            for m in range(2):
                wcat[pl.ds(start, step), m * hid + h * step : m * hid + (h + 1) * step] = slots[
                    m, inv_s[m, h * wb + w]
                ]
            wdn[h * step : (h + 1) * step, pl.ds(start, step)] = slots[2, inv_s[2, h * wb + w]]
        return carry

    lax.fori_loop(0, wb, lay, 0)

    def assemble(gathered, whole):
        parts = [gathered[i].astype(f32) for i in range(n_hid)]
        whole[...] = jnp.concatenate(parts, axis=0).astype(bf16)

    local[0].wait()
    arrive(xg, *hid_axis, x_s, x_r)
    assemble(xg, x_v)
    ranks = dot_nt(x_v[...], a2[...])
    rbuf[me_w] = ranks
    low_rank = wide(dot(two_parts(ranks), bcat[...]))
    fbuf[me_w] = dot(x_v[...], wcat[...]) + adapter_scale * low_rank
    sent += send(lambda peer: fbuf.at[me_w], fbuf, *wid_axis, f_s, f_r)
    sent += send(lambda peer: rbuf.at[me_w], rbuf, *wid_axis, r_s, r_r)

    local[1].wait()
    arrive(yg, *hid_axis, y_s, y_r)
    assemble(yg, y_v)
    grad_rank = dot_nt(y_v[...], bd_v[...])
    back_low = wide(dot(two_parts(grad_rank), ad_v[...]))
    hbuf[me_w] = (dot_nt(y_v[...], wdn[...]) + adapter_scale * back_low).astype(bf16)
    sent += send(lambda peer: hbuf.at[me_w], hbuf, *wid_axis, h_s, h_r)

    arrive(fbuf, *wid_axis, f_s, f_r)
    arrive(rbuf, *wid_axis, r_s, r_r)
    both = sum(fbuf[i] for i in range(n_wid))
    ranks = sum(rbuf[i] for i in range(n_wid))
    gate, up = both[:, :hid], both[:, hid:]
    sig = jax.nn.sigmoid(gate)
    act = gate * sig
    hidden = (act * up).astype(bf16)
    dbuf[me_h] = dot_nt(hidden, ad_v[...])
    sent += send(lambda peer: dbuf.at[me_h], dbuf, *hid_axis, d_s, d_r)
    slope = up * sig * (1.0 + gate * (1.0 - sig))
    arrive(hbuf, *wid_axis, h_s, h_r)
    hidden_grad = sum(hbuf[i].astype(f32) for i in range(n_wid))
    grads = jnp.concatenate(
        [(hidden_grad * slope).astype(bf16), (hidden_grad * act).astype(bf16)], axis=1
    )
    backs = two_parts(adapter_scale * dot_nt(grads, bcat[...]))
    total = dot_nt(grads, wcat[...]) + wide(dot(backs, a2[...]))
    for i in range(n_hid):
        sbuf[i] = total[i * own : (i + 1) * own].astype(bf16)
    acc[...] = total.reshape(n_hid, own, width)
    sent += send(lambda peer: sbuf.at[peer], tbuf, *hid_axis, t_s, t_r)

    ranks_t = adapter_scale * ranks.T
    gbuf[me_d, :, :hid] = wide(dot(two_parts(ranks_t[:rank]), grads[:, :hid]))
    gbuf[me_d, :, hid:] = wide(dot(two_parts(ranks_t[rank:]), grads[:, hid:]))
    sent += send(lambda peer: gbuf.at[me_d], gbuf, *dat_axis, g_s, g_r)

    arrive(dbuf, *hid_axis, d_s, d_r)
    down_rank = adapter_scale * sum(dbuf[i] for i in range(n_hid)).T
    ebuf[me_d] = wide(dot(two_parts(down_rank), y_v[...]))
    sent += send(lambda peer: ebuf.at[me_d], ebuf, *dat_axis, e_s, e_r)

    arrive(gbuf, *dat_axis, g_s, g_r)
    summed = sum(gbuf[i] for i in range(n_dat))
    gate_out[...] = summed[:, :hid]
    up_out[...] = summed[:, hid:]
    arrive(tbuf, *hid_axis, t_s, t_r)
    mine = acc[me_h]
    for peer in peers(me_h, n_hid):
        mine = mine + tbuf[peer].astype(f32)
    tok_out[...] = mine.astype(bf16)
    arrive(ebuf, *dat_axis, e_s, e_r)
    down_out[...] = sum(ebuf[i] for i in range(n_dat))
    for copy in sent:
        copy.wait_send()


def hand_out(*refs):
    sems = refs[8]
    copies = [pltpu.make_async_copy(refs[i], refs[i + 4], sems.at[i]) for i in range(4)]
    for copy in copies:
        copy.start()
    for copy in copies:
        copy.wait()


def shards(
    n_hid, n_wid, n_dat,
    tokens, output_gradient,
    gate_weight_blocks, gate_block_places,
    up_weight_blocks, up_block_places,
    down_weight_blocks, down_block_places,
    gate_adapter_first, gate_adapter_second,
    up_adapter_first, up_adapter_second,
    down_adapter_first, down_adapter_second,
):
    own, width = tokens.shape
    rows = own * n_hid
    cap, step = gate_weight_blocks.shape[2], gate_weight_blocks.shape[3]
    rank, hid = gate_adapter_second.shape
    positions = (hid // step) * (width // step)
    lanes = -(-positions // 128) * 128
    any_spec = pl.BlockSpec(memory_space=pl.ANY)
    vmem_spec = pl.BlockSpec(memory_space=pltpu.VMEM)
    V = pltpu.VMEM
    D = pltpu.SemaphoreType.DMA

    shapes = (
        jax.ShapeDtypeStruct((own, width), bf16),
        jax.ShapeDtypeStruct((rank, hid), f32),
        jax.ShapeDtypeStruct((rank, hid), f32),
        jax.ShapeDtypeStruct((rank, width), f32),
    )

    def sems(n):
        return [D((max(n - 1, 1),)), D((n,))]

    results = pl.pallas_call(
        functools.partial(kernel, n_hid, n_wid, n_dat),
        out_shape=shapes,
        in_specs=[any_spec] * 14,
        out_specs=(vmem_spec,) * 4,
        scratch_shapes=[
            V((3, cap + 1, step, step), bf16),
            pltpu.SMEM((3, 1, cap), jnp.int32),
            V((8, lanes), jnp.int32),
            pltpu.SMEM((8, lanes), jnp.int32),
            V((width, 2 * hid), bf16),
            V((hid, width), bf16),
            V((2 * rank, 2 * hid), bf16),
            V((2 * rank, width), bf16),
            V((rank, hid), bf16),
            V((rank, width), bf16),
            V((n_hid, own, width), bf16),
            V((n_hid, own, width), bf16),
            V((rows, width), bf16),
            V((rows, width), bf16),
            V((n_wid, rows, 2 * hid), f32),
            V((n_wid, rows, 2 * rank), f32),
            V((n_wid, rows, hid), bf16),
            V((n_hid, own, width), bf16),
            V((n_hid, own, width), bf16),
            V((n_hid, rows, rank), f32),
            V((n_dat, rank, 2 * hid), f32),
            V((n_dat, rank, width), f32),
            V((n_hid, own, width), f32),
            D((15,)),
            *sems(n_hid), *sems(n_hid), *sems(n_wid), *sems(n_wid), *sems(n_wid),
            *sems(n_hid), *sems(n_hid), *sems(n_dat), *sems(n_dat),
        ],
        compiler_params=pltpu.CompilerParams(
            collective_id=0, has_side_effects=True, vmem_limit_bytes=40 * 1024 * 1024
        ),
    )(
        *(
            pltpu.with_memory_space_constraint(operand, pltpu.HBM)
            for operand in (
                tokens, output_gradient,
                gate_weight_blocks, up_weight_blocks, down_weight_blocks,
                gate_block_places, up_block_places, down_block_places,
                gate_adapter_first.T, gate_adapter_second,
                up_adapter_first.T, up_adapter_second,
                down_adapter_first.T, down_adapter_second,
            )
        ),
    )
    return pl.pallas_call(
        hand_out,
        out_shape=shapes,
        in_specs=[vmem_spec] * 4,
        out_specs=(any_spec,) * 4,
        scratch_shapes=[D((4,))],
    )(*(pltpu.with_memory_space_constraint(result, pltpu.VMEM) for result in results))


def solution(mesh):
    sizes = (mesh.shape["hid"], mesh.shape["wid"], mesh.shape["dat"])
    return jax.shard_map(
        functools.partial(shards, *sizes),
        mesh=mesh,
        in_specs=(
            P(("grp", "hid", "dat"), "wid"),
            P(("grp", "hid", "dat"), "wid"),
            P("hid", "wid", None, None, None),
            P("hid", "wid", None),
            P("hid", "wid", None, None, None),
            P("hid", "wid", None),
            P("hid", "wid", None, None, None),
            P("hid", "wid", None),
            P("wid", None),
            P(None, "hid"),
            P("wid", None),
            P(None, "hid"),
            P("hid", None),
            P(None, "wid"),
        ),
        out_specs=(
            P(("grp", "hid", "dat"), "wid"),
            P("grp", "hid"),
            P("grp", "hid"),
            P("grp", "wid"),
        ),
        check_vma=False,
    )
```

```python
import functools

import jax
import jax.numpy as jnp
from jax import lax
from jax.experimental import pallas as pl
from jax.experimental.pallas import tpu as pltpu
from jax.sharding import PartitionSpec as P

adapter_scale = 2.0
MESH = pl.DeviceIdType.MESH
bf16, f32 = jnp.bfloat16, jnp.float32


def dot(left, right):
    return jnp.dot(left, right, preferred_element_type=f32)


def dot_nt(left, right):
    return lax.dot_general(left, right, (((1,), (1,)), ((), ())), preferred_element_type=f32)


def two_parts(value):
    high = value.astype(bf16)
    low = (value - high.astype(f32)).astype(bf16)
    return jnp.concatenate([high, low], axis=0)


def wide(product):
    half = product.shape[0] // 2
    return product[:half] + product[half:]


def kernel(
    n_hid, n_wid, n_dat,
    tok, dy, wg, wu, wd, pg, pu, pd, ag, bg, au, bu, ad, bd,
    tok_out, gate_out, up_out, down_out,
    slots, places, inv_v, inv_s, wback, wcat, wdn, bcat, a2, ad_v, bd_v,
    xg, yg, x_v, y_v, fbuf, rbuf, hbuf, sbuf, tbuf, dbuf, gbuf, ebuf, acc,
    local_sem, x_s, x_r, y_s, y_r, f_s, f_r, r_s, r_r, h_s, h_r, t_s, t_r, d_s, d_r, g_s, g_r, e_s, e_r,
):
    me_h, me_w, me_d = lax.axis_index("hid"), lax.axis_index("wid"), lax.axis_index("dat")
    own, width = tok.shape
    rows = own * n_hid
    cap, step = wg.shape[2], wg.shape[3]
    hid = bg.shape[1]
    rank = bg.shape[0]
    hb, wb = hid // step, width // step

    def peers(me, n):
        return [lax.rem(me + d, n) for d in range(1, n)]

    groups = (("hid", me_h, n_hid), ("wid", me_w, n_wid), ("dat", me_d, n_dat))
    barrier = pltpu.get_barrier_semaphore()
    for axis, me, n in groups:
        for peer in peers(me, n):
            pl.semaphore_signal(barrier, inc=1, device_id={axis: peer}, device_id_type=MESH)

    pairs = [
        (tok, xg.at[me_h]),
        (dy, yg.at[me_h]),
        (wg.at[0, 0], slots.at[0, pl.ds(0, cap)]),
        (wu.at[0, 0], slots.at[1, pl.ds(0, cap)]),
        (wd.at[0, 0], slots.at[2, pl.ds(0, cap)]),
        (ag, a2.at[pl.ds(0, rank)]),
        (au, a2.at[pl.ds(rank, rank)]),
        (bg, bcat.at[pl.ds(0, rank), pl.ds(0, hid)]),
        (bu, bcat.at[pl.ds(rank, rank), pl.ds(hid, hid)]),
        (ad, ad_v),
        (bd, bd_v),
        (pg.at[0], places.at[0]),
        (pu.at[0], places.at[1]),
        (pd.at[0], places.at[2]),
    ]
    local = [pltpu.make_async_copy(s, d, local_sem.at[i]) for i, (s, d) in enumerate(pairs)]
    for copy in local:
        copy.start()

    pl.semaphore_wait(barrier, n_hid + n_wid + n_dat - 3)

    def send(source, buf, axis, me, n, send_sem, recv_sem):
        copies = []
        for d, peer in enumerate(peers(me, n)):
            copy = pltpu.make_async_remote_copy(
                src_ref=source(peer), dst_ref=buf.at[me],
                send_sem=send_sem.at[d], recv_sem=recv_sem.at[me],
                device_id={axis: peer}, device_id_type=MESH,
            )
            copy.start()
            copies.append(copy)
        return copies

    def arrive(buf, axis, me, n, send_sem, recv_sem):
        for d, peer in enumerate(peers(me, n)):
            pltpu.make_async_remote_copy(
                src_ref=buf.at[peer], dst_ref=buf.at[peer],
                send_sem=send_sem.at[d], recv_sem=recv_sem.at[peer],
                device_id={axis: peer}, device_id_type=MESH,
            ).wait_recv()

    hid_axis, wid_axis, dat_axis = groups
    sent = send(lambda peer: tok, xg, *hid_axis, x_s, x_r)
    sent += send(lambda peer: dy, yg, *hid_axis, y_s, y_r)

    lanes = inv_v.shape[1]
    lane = lax.broadcasted_iota(jnp.int32, (8, lanes), 1)
    row = lax.broadcasted_iota(jnp.int32, (8, lanes), 0)
    inverse = jnp.full((8, lanes), cap, jnp.int32)
    for m in range(3):
        local[11 + m].wait()
        mine = jnp.where(row == m, lane, -1)
        for k in range(cap):
            inverse = jnp.where(mine == places[m, 0, k], k, inverse)
    inv_v[...] = inverse
    inv_copy = pltpu.make_async_copy(inv_v, inv_s, local_sem.at[len(pairs)])
    inv_copy.start()
    for m in range(3):
        slots[m, cap] = jnp.zeros((step, step), bf16)
    bcat[:rank, hid:] = jnp.zeros((rank, hid), bf16)
    bcat[rank:, :hid] = jnp.zeros((rank, hid), bf16)
    for copy in local[5:11]:
        copy.wait()
    inv_copy.wait()
    for copy in local[2:5]:
        copy.wait()

    def lay(w, carry):
        start = pl.multiple_of(w * step, step)
        for h in range(hb):
            for m in range(2):
                wcat[pl.ds(start, step), m * hid + h * step : m * hid + (h + 1) * step] = slots[
                    m, inv_s[m, h * wb + w]
                ]
            wdn[pl.ds(start, step), h * step : (h + 1) * step] = slots[2, inv_s[2, h * wb + w]].T
        return carry

    lax.fori_loop(0, wb, lay, 0)

    def lay_back(w, carry):
        start = pl.multiple_of(w * step, step)
        for h in range(hb):
            for m in (0,):
                wback[m * hid + h * step : m * hid + (h + 1) * step, pl.ds(start, step)] = wcat[
                    pl.ds(start, step), m * hid + h * step : m * hid + (h + 1) * step
                ].T
        return carry

    lax.fori_loop(0, wb, lay_back, 0)

    def assemble(gathered, whole):
        parts = [gathered[i].astype(f32) for i in range(n_hid)]
        whole[...] = jnp.concatenate(parts, axis=0).astype(bf16)

    local[0].wait()
    arrive(xg, *hid_axis, x_s, x_r)
    assemble(xg, x_v)
    ranks = dot_nt(x_v[...], a2[...])
    rbuf[me_w] = ranks
    low_rank = wide(dot(two_parts(ranks), bcat[...]))
    fbuf[me_w] = dot(x_v[...], wcat[...]) + adapter_scale * low_rank
    sent += send(lambda peer: fbuf.at[me_w], fbuf, *wid_axis, f_s, f_r)
    sent += send(lambda peer: rbuf.at[me_w], rbuf, *wid_axis, r_s, r_r)

    local[1].wait()
    arrive(yg, *hid_axis, y_s, y_r)
    assemble(yg, y_v)
    grad_rank = dot_nt(y_v[...], bd_v[...])
    back_low = wide(dot(two_parts(grad_rank), ad_v[...]))
    hbuf[me_w] = (dot(y_v[...], wdn[...]) + adapter_scale * back_low).astype(bf16)
    sent += send(lambda peer: hbuf.at[me_w], hbuf, *wid_axis, h_s, h_r)

    def lay_back_up(w, carry):
        start = pl.multiple_of(w * step, step)
        for h in range(hb):
            for m in (1,):
                wback[m * hid + h * step : m * hid + (h + 1) * step, pl.ds(start, step)] = wcat[
                    pl.ds(start, step), m * hid + h * step : m * hid + (h + 1) * step
                ].T
        return carry

    lax.fori_loop(0, wb, lay_back_up, 0)

    arrive(fbuf, *wid_axis, f_s, f_r)
    arrive(rbuf, *wid_axis, r_s, r_r)
    both = sum(fbuf[i] for i in range(n_wid))
    ranks = sum(rbuf[i] for i in range(n_wid))
    gate, up = both[:, :hid], both[:, hid:]
    sig = jax.nn.sigmoid(gate)
    act = gate * sig
    hidden = (act * up).astype(bf16)
    dbuf[me_h] = dot_nt(hidden, ad_v[...])
    sent += send(lambda peer: dbuf.at[me_h], dbuf, *hid_axis, d_s, d_r)
    slope = up * sig * (1.0 + gate * (1.0 - sig))
    arrive(hbuf, *wid_axis, h_s, h_r)
    hidden_grad = sum(hbuf[i].astype(f32) for i in range(n_wid))
    grads = jnp.concatenate(
        [(hidden_grad * slope).astype(bf16), (hidden_grad * act).astype(bf16)], axis=1
    )
    backs = two_parts(adapter_scale * dot_nt(grads, bcat[...]))
    total = dot(grads, wback[...]) + wide(dot(backs, a2[...]))
    for i in range(n_hid):
        sbuf[i] = total[i * own : (i + 1) * own].astype(bf16)
    acc[...] = total.reshape(n_hid, own, width)
    sent += send(lambda peer: sbuf.at[peer], tbuf, *hid_axis, t_s, t_r)

    ranks_t = adapter_scale * ranks.T
    gbuf[me_d, :, :hid] = wide(dot(two_parts(ranks_t[:rank]), grads[:, :hid]))
    gbuf[me_d, :, hid:] = wide(dot(two_parts(ranks_t[rank:]), grads[:, hid:]))
    sent += send(lambda peer: gbuf.at[me_d], gbuf, *dat_axis, g_s, g_r)

    arrive(dbuf, *hid_axis, d_s, d_r)
    down_rank = adapter_scale * sum(dbuf[i] for i in range(n_hid)).T
    ebuf[me_d] = wide(dot(two_parts(down_rank), y_v[...]))
    sent += send(lambda peer: ebuf.at[me_d], ebuf, *dat_axis, e_s, e_r)

    arrive(gbuf, *dat_axis, g_s, g_r)
    summed = sum(gbuf[i] for i in range(n_dat))
    gate_out[...] = summed[:, :hid]
    up_out[...] = summed[:, hid:]
    arrive(tbuf, *hid_axis, t_s, t_r)
    mine = acc[me_h]
    for peer in peers(me_h, n_hid):
        mine = mine + tbuf[peer].astype(f32)
    tok_out[...] = mine.astype(bf16)
    arrive(ebuf, *dat_axis, e_s, e_r)
    down_out[...] = sum(ebuf[i] for i in range(n_dat))
    for copy in sent:
        copy.wait_send()


def hand_out(*refs):
    sems = refs[8]
    copies = [pltpu.make_async_copy(refs[i], refs[i + 4], sems.at[i]) for i in range(4)]
    for copy in copies:
        copy.start()
    for copy in copies:
        copy.wait()


def shards(
    n_hid, n_wid, n_dat,
    tokens, output_gradient,
    gate_weight_blocks, gate_block_places,
    up_weight_blocks, up_block_places,
    down_weight_blocks, down_block_places,
    gate_adapter_first, gate_adapter_second,
    up_adapter_first, up_adapter_second,
    down_adapter_first, down_adapter_second,
):
    own, width = tokens.shape
    rows = own * n_hid
    cap, step = gate_weight_blocks.shape[2], gate_weight_blocks.shape[3]
    rank, hid = gate_adapter_second.shape
    positions = (hid // step) * (width // step)
    lanes = -(-positions // 128) * 128
    any_spec = pl.BlockSpec(memory_space=pl.ANY)
    vmem_spec = pl.BlockSpec(memory_space=pltpu.VMEM)
    V = pltpu.VMEM
    D = pltpu.SemaphoreType.DMA

    shapes = (
        jax.ShapeDtypeStruct((own, width), bf16),
        jax.ShapeDtypeStruct((rank, hid), f32),
        jax.ShapeDtypeStruct((rank, hid), f32),
        jax.ShapeDtypeStruct((rank, width), f32),
    )

    def sems(n):
        return [D((max(n - 1, 1),)), D((n,))]

    results = pl.pallas_call(
        functools.partial(kernel, n_hid, n_wid, n_dat),
        out_shape=shapes,
        in_specs=[any_spec] * 14,
        out_specs=(vmem_spec,) * 4,
        scratch_shapes=[
            V((3, cap + 1, step, step), bf16),
            pltpu.SMEM((3, 1, cap), jnp.int32),
            V((8, lanes), jnp.int32),
            pltpu.SMEM((8, lanes), jnp.int32),
            V((2 * hid, width), bf16),
            V((width, 2 * hid), bf16),
            V((width, hid), bf16),
            V((2 * rank, 2 * hid), bf16),
            V((2 * rank, width), bf16),
            V((rank, hid), bf16),
            V((rank, width), bf16),
            V((n_hid, own, width), bf16),
            V((n_hid, own, width), bf16),
            V((rows, width), bf16),
            V((rows, width), bf16),
            V((n_wid, rows, 2 * hid), f32),
            V((n_wid, rows, 2 * rank), f32),
            V((n_wid, rows, hid), bf16),
            V((n_hid, own, width), bf16),
            V((n_hid, own, width), bf16),
            V((n_hid, rows, rank), f32),
            V((n_dat, rank, 2 * hid), f32),
            V((n_dat, rank, width), f32),
            V((n_hid, own, width), f32),
            D((15,)),
            *sems(n_hid), *sems(n_hid), *sems(n_wid), *sems(n_wid), *sems(n_wid),
            *sems(n_hid), *sems(n_hid), *sems(n_dat), *sems(n_dat),
        ],
        compiler_params=pltpu.CompilerParams(
            collective_id=0, has_side_effects=True, vmem_limit_bytes=40 * 1024 * 1024
        ),
    )(
        *(
            pltpu.with_memory_space_constraint(operand, pltpu.HBM)
            for operand in (
                tokens, output_gradient,
                gate_weight_blocks, up_weight_blocks, down_weight_blocks,
                gate_block_places, up_block_places, down_block_places,
                gate_adapter_first.T, gate_adapter_second,
                up_adapter_first.T, up_adapter_second,
                down_adapter_first.T, down_adapter_second,
            )
        ),
    )
    return pl.pallas_call(
        hand_out,
        out_shape=shapes,
        in_specs=[vmem_spec] * 4,
        out_specs=(any_spec,) * 4,
        scratch_shapes=[D((4,))],
    )(*(pltpu.with_memory_space_constraint(result, pltpu.VMEM) for result in results))


def solution(mesh):
    sizes = (mesh.shape["hid"], mesh.shape["wid"], mesh.shape["dat"])
    return jax.shard_map(
        functools.partial(shards, *sizes),
        mesh=mesh,
        in_specs=(
            P(("grp", "hid", "dat"), "wid"),
            P(("grp", "hid", "dat"), "wid"),
            P("hid", "wid", None, None, None),
            P("hid", "wid", None),
            P("hid", "wid", None, None, None),
            P("hid", "wid", None),
            P("hid", "wid", None, None, None),
            P("hid", "wid", None),
            P("wid", None),
            P(None, "hid"),
            P("wid", None),
            P(None, "hid"),
            P("hid", None),
            P(None, "wid"),
        ),
        out_specs=(
            P(("grp", "hid", "dat"), "wid"),
            P("grp", "hid"),
            P("grp", "hid"),
            P("grp", "wid"),
        ),
        check_vma=False,
    )
```
